32 devices in a mesh: row: 8 (over y, x, core), col: 4 (over z).
Axes of the slice: x: 2, y: 2, z: 4, core: 2. Of those that a mesh axis runs over, the one named last changes fastest.
Arguments:
- child_tiles: float32 [896, 256, 128], P(('row', 'col')), may hold values from -2.5 to 2.5
- tile_dest: int32 [896], P(('row', 'col')), may hold values from 0 to 3071, as said below
- tile_mask: int32 [896, 256], P(('row', 'col')), may hold values 0 or 1
- tile_count: int32 [32], P(('row', 'col')), may hold values from 21 to 28, as said below
- front_diagonal: float32 [2, 1024], P(None, 'col'), may hold values from 200 to 400
Outputs:
- front_out: float32 [49152, 2, 1024], P('row', None, 'col')
The draws below stay inside these ranges and needn't reach their ends.
Inputs may be any that keep to these rules, and one draw needn't show every extreme that they name: tile_dest[i] = r * 16 + t names front rows r * 256 onward and slab columns t * 128 onward; of the 28 tiles of one device at most 2 name tiles that lie on any one device of front_out's placement, and that most is reached. Tile i * 28 + m is live when m < tile_count[i].
All inputs are finite; a program needn't handle non-finite values. No bound on the sum of `tile_mask` on one device may be relied on, other than what follows from the above.
Results may differ from the reference program's by a relative error of at most 0.0001.
Values sent between devices are 32-bit elements; how exact they have to be, the bound alone decides.
A program may use at most 192 MiB of HBM per device.

```python
import jax
import jax.numpy as jnp
from jax import lax

NF = 49152
PB = 256
TR = 256
CAP = 2
CB = 2
TC = 128
NCT = 16
KT = 28
N_ROW = 8
N_COL = 4
DEVICES = 32


def draw_tile_dest(key, part):
    base_key = jax.random.fold_in(key, 11)
    k_hot, k_pick, k_row, k_blk, k_half = jax.random.split(base_key, 5)
    slot_count = DEVICES * CAP
    heavy_set = jax.random.permutation(k_hot, DEVICES)[:DEVICES // 8]
    heavy_flag = jnp.zeros((DEVICES,), jnp.int32).at[heavy_set].set(1)
    slot_owner = jnp.arange(slot_count, dtype=jnp.int32) // CAP
    scores = jax.random.randint(k_pick, (DEVICES, slot_count), 0, 4096) + heavy_flag[slot_owner][None, :] * 4096
    scores = scores * slot_count + jnp.arange(slot_count, dtype=jnp.int32)[None, :]
    chosen = lax.top_k(scores, KT)[1]
    owner_dev = chosen // CAP
    owner_row = owner_dev // N_COL
    owner_col = owner_dev % N_COL
    row_tiles = NF // (N_ROW * TR)
    row_tile = owner_row * row_tiles + jax.random.randint(k_row, (DEVICES, KT), 0, row_tiles)
    col_block = owner_col + N_COL * jax.random.randint(k_blk, (DEVICES, KT), 0, CB)
    col_half = jax.random.randint(k_half, (DEVICES, KT), 0, PB // TC)
    result = row_tile * NCT + col_block * (PB // TC) + col_half
    return result.reshape(DEVICES * KT).astype(jnp.int32)


def draw_tile_count(key, part):
    base_key = jax.random.fold_in(key, 23)
    k_count, k_full = jax.random.split(base_key, 2)
    counts = jax.random.randint(k_count, (DEVICES,), 3 * KT // 4, KT + 1)
    full_at = jax.random.randint(k_full, (), 0, DEVICES)
    return counts.at[full_at].set(KT).astype(jnp.int32)


def touch_ends(entries, rng, smallest, high):
    longest = entries.shape.index(max(entries.shape))
    spots = []
    for shift in (0, 1):
        where = [jax.random.randint(jax.random.fold_in(rng, axis), (), 0, length) for axis, length in enumerate(entries.shape)]
        where[longest] = (where[longest] + shift) % entries.shape[longest]
        spots.append(tuple(where))
    return entries.at[spots[0]].set(smallest).at[spots[1]].set(high)


def level_of(own_key, dims, pieces, low, largest):
    def one(dim, parts):
        heights = jax.random.uniform(jax.random.fold_in(jax.random.fold_in(own_key, 6), dim), (parts,), jnp.float32, low / len(pieces), largest / len(pieces))
        return jnp.repeat(jnp.exp(heights), dims[dim] // parts).reshape((-1,) + (1,) * (len(dims) - dim - 1))

    factor_of = one(*pieces[0])
    for cut in pieces[1:]:
        factor_of = factor_of * one(*cut)
    return factor_of


def gaussian(own_key, extent, deviation, most, pieces=(), kind=jnp.bfloat16):
    values = deviation * jax.random.normal(own_key, extent, jnp.float32)
    if pieces:
        values = values * level_of(own_key, extent, pieces, -0.22, 0.18)
    return jnp.clip(values, -most, most).astype(kind)


def setup_inputs(seed: int = 0) -> dict:
    keys = jax.random.split(jax.random.key(seed), 6)
    child_tiles = gaussian(keys[0], (DEVICES * KT, TR, TC), 1.0, 2.5, ((0, 32),), jnp.float32)
    tile_dest = draw_tile_dest(jax.random.fold_in(keys[5], 71), 0)
    tile_mask = touch_ends((jax.random.randint(keys[2], (DEVICES * KT, TR), 0, 4) < 3).astype(jnp.int32), jax.random.fold_in(keys[2], 1), 0, 1)
    tile_count = draw_tile_count(jax.random.fold_in(keys[5], 71), 0)
    front_diagonal = jnp.clip(200.0 + 200.0 * jax.random.uniform(keys[4], (CB, N_COL * PB), jnp.float32) ** level_of(keys[4], (CB, N_COL * PB), ((1, 4),), -0.2, 0.2), 200.0, 400.0)
    return dict(child_tiles=child_tiles, tile_dest=tile_dest, tile_mask=tile_mask, tile_count=tile_count, front_diagonal=front_diagonal)


def reference(child_tiles, tile_dest, tile_mask, tile_count, front_diagonal):
    col_tiles = CB * N_COL * PB // TC
    tile_total = NF // TR * col_tiles
    width = col_tiles * TC
    positions = jnp.arange(DEVICES * KT, dtype=jnp.int32)
    is_live = positions % KT < tile_count[positions // KT]
    targets = jnp.where(is_live, tile_dest, tile_total).astype(jnp.int32)
    masked = child_tiles * tile_mask.astype(jnp.float32)[:, :, None]
    summed = jax.ops.segment_sum(masked, targets, num_segments=tile_total + 1)[:tile_total]
    assembled = summed.reshape(NF // TR, col_tiles, TR, TC).transpose(0, 2, 1, 3).reshape(NF, width)
    diag_flat = front_diagonal.reshape(width)
    columns = jnp.arange(width, dtype=jnp.int32)
    assembled = assembled.at[columns, columns].add(diag_flat)
    row_ids = jnp.arange(NF, dtype=jnp.int32)[:, None]
    for section in range(2):
        lower_edge = section * PB
        upper_edge = lower_edge + PB
        pivot = assembled[lower_edge:upper_edge, lower_edge:upper_edge]
        factor = jnp.linalg.cholesky(0.5 * (pivot + pivot.T))
        panel_raw = assembled[:, lower_edge:upper_edge]
        solved = jax.scipy.linalg.solve_triangular(factor, panel_raw.T, lower=True).T
        lower_panel = jnp.where(row_ids < lower_edge, jnp.zeros_like(solved), solved)
        lower_panel = lower_panel.at[lower_edge:upper_edge].set(factor)
        update_term = jnp.dot(lower_panel, lower_panel[upper_edge:width].T, precision=lax.Precision.HIGHEST)
        assembled = assembled.at[:, upper_edge:].add(-update_term)
        assembled = assembled.at[:, lower_edge:upper_edge].set(lower_panel)
    return assembled.reshape(NF, CB, N_COL * PB)
```

```python
import functools

import jax
import jax.numpy as jnp
from jax import lax
from jax.experimental import pallas as pl
from jax.experimental.pallas import tpu as pltpu
from jax.sharding import PartitionSpec as P

NF = 49152
CAP = 2
SECTIONS = 2
HI = lax.Precision.HIGHEST
MESH = pl.DeviceIdType.MESH


def mm(a, b):
    return jnp.dot(a, b, precision=HI)


def add_tiles(order_ref, start_ref, arrived_ref, position, shape):
    first = start_ref[position]
    last = start_ref[position + 1]
    return lax.fori_loop(
        first, last, lambda i, acc: acc + arrived_ref[order_ref[i]], jnp.zeros(shape, jnp.float32)
    )


def diagonal_tile(diag_row, half, shape):
    rows = lax.broadcasted_iota(jnp.int32, shape, 0)
    cols = lax.broadcasted_iota(jnp.int32, shape, 1) + half * shape[1]
    return jnp.where(rows == cols, diag_row, 0.0)


def panel_kernel(halves, order_ref, start_ref, where_ref, arrived_ref, diag_ref, out_ref):
    step = pl.program_id(0)
    shape = out_ref.shape[2:]
    base = where_ref[0] + step

    @pl.when(where_ref[1] < SECTIONS)
    def _():
        for half in range(halves):
            out_ref[0, half] = add_tiles(
                order_ref, start_ref, arrived_ref, step * where_ref[2] + half, shape
            )

        @pl.when(base == where_ref[1])
        def _():
            for half in range(halves):
                diag_row = diag_ref[0:1, half * shape[1] : (half + 1) * shape[1]]
                out_ref[0, half] += diagonal_tile(diag_row, half, shape)


def chain_kernel(n_row, n_col, col_blocks, pieces, own_ref, all_ref, rows_ref, copy_sem, send_sem, recv_sem, rsend_sem, rrecv_sem):
    row = lax.axis_index("row")
    col = lax.axis_index("col")
    row_tiles = own_ref.shape[0]
    per = row_tiles // pieces
    barrier = pltpu.get_barrier_semaphore()
    for step in (1, -1):
        inside = (col < n_col - 1) if step == 1 else (col > 0)

        @pl.when(inside)
        def _():
            pl.semaphore_signal(
                barrier, inc=1, device_id={"col": col + step}, device_id_type=MESH
            )

    for shift in range(1, n_row):
        pl.semaphore_signal(
            barrier,
            inc=1,
            device_id={"row": lax.rem(row + shift, n_row)},
            device_id_type=MESH,
        )

    at_end = jnp.logical_or(col == 0, col == n_col - 1)

    @pl.when(at_end)
    def _():
        pl.semaphore_wait(barrier, n_row)

    @pl.when(jnp.logical_not(at_end))
    def _():
        pl.semaphore_wait(barrier, n_row + 1)

    def part(ref, piece):
        return ref.at[pl.ds(piece * per, per)]

    def hop(section, piece, step, from_own):
        target = all_ref.at[section]
        source = own_ref if from_own else target
        way = 0 if step == 1 else 1
        return pltpu.make_async_remote_copy(
            src_ref=part(source, piece),
            dst_ref=part(target, piece),
            send_sem=send_sem.at[section, way, piece],
            recv_sem=recv_sem.at[section, piece],
            device_id={"col": col + step},
            device_id_type=MESH,
        )

    def local(section):
        return pltpu.make_async_copy(own_ref, all_ref.at[section], copy_sem)

    for section in range(SECTIONS):

        @pl.when(col == section)
        def _():
            local(section).start()
            for piece in range(pieces):
                hop(section, piece, 1, True).start()
                if section > 0:
                    hop(section, piece, -1, True).start()
            local(section).wait()

    def row_copy(block, section, shift):
        tile = block * n_col + col
        return pltpu.make_async_remote_copy(
            src_ref=all_ref.at[section, lax.rem(tile, row_tiles)],
            dst_ref=rows_ref.at[block, section],
            send_sem=rsend_sem.at[block, section, shift],
            recv_sem=rrecv_sem.at[block, section],
            device_id={"row": lax.rem(row + shift, n_row)},
            device_id_type=MESH,
        )

    def row_local(block, section):
        tile = block * n_col + col
        return pltpu.make_async_copy(
            all_ref.at[section, lax.rem(tile, row_tiles)],
            rows_ref.at[block, section],
            rsend_sem.at[block, section, 0],
        )

    def owner(block):
        return row == (block * n_col + col) // row_tiles

    needed = min(col_blocks * n_col, row_tiles)
    send_rows_at = -(-needed // per) - 1
    for piece in range(pieces):
        for section in range(SECTIONS):

            @pl.when(col != section)
            def _():
                hop(section, piece, 1, False).wait_recv()

            if section < n_col - 1:

                @pl.when(jnp.logical_and(col > section, col < n_col - 1))
                def _():
                    hop(section, piece, 1, False).start()

            if section > 1:

                @pl.when(jnp.logical_and(col < section, col > 0))
                def _():
                    hop(section, piece, -1, False).start()

        if piece == send_rows_at:
            for block in range(col_blocks):

                @pl.when(owner(block))
                def _():
                    for section in range(SECTIONS):
                        for shift in range(1, n_row):
                            row_copy(block, section, shift).start()
                        row_local(block, section).start()

    for block in range(col_blocks):

        @pl.when(owner(block))
        def _():
            for section in range(SECTIONS):
                for shift in range(1, n_row):
                    row_copy(block, section, shift).wait_send()
                row_local(block, section).wait()

        @pl.when(jnp.logical_not(owner(block)))
        def _():
            for section in range(SECTIONS):
                row_copy(block, section, 1).wait_recv()

    for section in range(SECTIONS):
        for piece in range(pieces):

            @pl.when(jnp.logical_and(col >= section, col < n_col - 1))
            def _():
                hop(section, piece, 1, False).wait_send()

            if section > 0:

                @pl.when(jnp.logical_and(col <= section, col > 0))
                def _():
                    hop(section, piece, -1, False).wait_send()


def final_kernel(col_blocks, halves, n_col, order_ref, start_ref, where_ref, arrived_ref, diag_ref, panels_ref, whi_ref, wlo_ref, top_ref, own_ref, out_ref, lhs_ref):
    step = pl.program_id(0)
    rows, lanes = arrived_ref.shape[1:]
    width = halves * lanes
    base = where_ref[0] + step
    for section in range(SECTIONS):
        for half in range(halves):
            low = section * width + half * lanes
            lhs_ref[:, low : low + lanes] = panels_ref[section, 0, half]

    @pl.when(base < SECTIONS)
    def _():
        lhs_ref[...] = top_ref[jnp.minimum(base, SECTIONS - 1)]

    lhs = lhs_ref[...]
    hi = lhs.astype(jnp.bfloat16)
    lo = (lhs - hi.astype(jnp.float32)).astype(jnp.bfloat16)
    whi = whi_ref[...]
    product = (
        jnp.dot(hi, wlo_ref[...], preferred_element_type=jnp.float32)
        + jnp.dot(lo, whi, preferred_element_type=jnp.float32)
    ) + jnp.dot(hi, whi, preferred_element_type=jnp.float32)
    panel_column = where_ref[1] < SECTIONS
    group = col_blocks * halves
    for block in range(col_blocks):
        for half in range(halves):
            low = block * width + half * lanes
            value = product[:, low : low + lanes]
            slot = half * col_blocks + block
            place = (pl.ds(slot, rows, stride=group), slice(None))

            def trailing():
                position = step * group + block * halves + half
                out_ref[place] = value + add_tiles(
                    order_ref, start_ref, arrived_ref, position, (rows, lanes)
                )

                @pl.when(base == block * n_col + where_ref[1])
                def _():
                    diag_row = diag_ref[block : block + 1, half * lanes : (half + 1) * lanes]
                    out_ref[place] = out_ref[place] + diagonal_tile(diag_row, half, (rows, lanes))

            if block > 0:
                trailing()
            else:
                pl.when(jnp.logical_not(panel_column))(trailing)

                @pl.when(panel_column)
                def _():
                    out_ref[place] = value

                @pl.when(jnp.logical_and(panel_column, base < SECTIONS))
                def _():
                    out_ref[place] = own_ref[
                        jnp.minimum(base, SECTIONS - 1), :, half * lanes : (half + 1) * lanes
                    ]


def on_device(n_row, n_col, child_tiles, tile_dest, tile_mask, tile_count, front_diagonal):
    devices = n_row * n_col
    row_index = lax.axis_index("row")
    col_index = lax.axis_index("col")
    tile_total, tile_rows, tile_cols = child_tiles.shape
    col_blocks, panel_width = front_diagonal.shape
    halves = panel_width // tile_cols
    local_rows = NF // n_row
    row_tiles = local_rows // tile_rows
    col_tiles = col_blocks * n_col * halves
    is_live = jnp.arange(tile_total, dtype=jnp.int32) < tile_count[0]
    row_tile = tile_dest // col_tiles
    col_tile = tile_dest % col_tiles
    col_block = col_tile // halves
    col_half = col_tile % halves
    owner_row = row_tile // row_tiles
    owner_dev = jnp.where(is_live, owner_row * n_col + col_block % n_col, devices)
    local_tile = (
        (row_tile - owner_row * row_tiles) * (col_blocks * halves)
        + col_block // n_col * halves
        + col_half
    )
    earlier = jnp.tril(jnp.ones((tile_total, tile_total), jnp.int32), -1)
    slot_rank = jnp.sum((owner_dev[:, None] == owner_dev[None, :]) * earlier, axis=1)
    position = jnp.where(is_live, owner_dev * CAP + slot_rank, devices * CAP)
    hit = position[None, :] == jnp.arange(devices * CAP, dtype=jnp.int32)[:, None]
    source = jnp.sum(
        hit * jnp.arange(tile_total, dtype=jnp.int32)[None, :], axis=1, dtype=jnp.int32
    )
    targets = jnp.sum(hit * (local_tile + 1)[None, :], axis=1, dtype=jnp.int32) - 1
    masked = child_tiles * tile_mask.astype(jnp.float32)[:, :, None]
    outgoing = masked[source]
    arrived_targets = lax.all_to_all(
        targets.reshape(devices, CAP), ("row", "col"), split_axis=0, concat_axis=0, tiled=True
    )
    arrived = lax.all_to_all(
        outgoing.reshape(devices, CAP, tile_rows, tile_cols),
        ("row", "col"),
        split_axis=0,
        concat_axis=0,
        tiled=True,
    ).reshape(-1, tile_rows, tile_cols)

    wide = SECTIONS * panel_width
    pivot_tiles = SECTIONS * halves
    in_pivot = is_live & (row_tile < SECTIONS) & (col_tile < pivot_tiles)
    pivot_slot = jnp.where(in_pivot, row_tile * pivot_tiles + col_tile, SECTIONS * pivot_tiles)
    pivot = jax.ops.segment_sum(masked, pivot_slot, num_segments=SECTIONS * pivot_tiles + 1)
    pivot = lax.psum(pivot[: SECTIONS * pivot_tiles], ("row", "col"))
    pivot = pivot.reshape(SECTIONS, pivot_tiles, tile_rows, tile_cols)
    pivot = pivot.transpose(0, 2, 1, 3).reshape(wide, wide)
    one_col = (jnp.arange(SECTIONS, dtype=jnp.int32) == col_index)[:, None] & (row_index == 0)
    diag = lax.psum(jnp.where(one_col, front_diagonal[0][None, :], 0.0), ("row", "col"))
    pivot = pivot + jnp.diag(diag.reshape(-1))
    eye = jnp.eye(panel_width, dtype=jnp.float32)
    b00 = pivot[:panel_width, :panel_width]
    b10 = pivot[panel_width:, :panel_width]
    b11 = pivot[panel_width:, panel_width:]
    b00 = 0.5 * (b00 + b00.T)
    b11 = 0.5 * (b11 + b11.T)
    l00 = jnp.linalg.cholesky(b00)
    x0 = jax.scipy.linalg.solve_triangular(l00, eye, lower=True)
    l10 = mm(b10, x0.T)
    l11 = jnp.linalg.cholesky(b11 - mm(l10, l10.T))
    x1 = jax.scipy.linalg.solve_triangular(l11, eye, lower=True)
    zero = jnp.zeros_like(eye)
    inverse = jnp.block([[x0, zero], [-mm(x1, mm(l10, x0)), x1]])
    full = jnp.block([[l00, zero], [l10, l11]])
    top = jnp.block([[b00, b10.T], [b10, b11]]).reshape(SECTIONS, tile_rows, wide)
    gram = mm(inverse.T, inverse)
    section_at = jnp.minimum(col_index, SECTIONS - 1) * panel_width
    own_top = lax.dynamic_slice_in_dim(full, section_at, panel_width, axis=1)
    own_top = own_top.reshape(SECTIONS, tile_rows, panel_width)
    own_weight = lax.dynamic_slice_in_dim(inverse, section_at, panel_width, axis=0).T

    n_local = row_tiles * col_blocks * halves
    flat = arrived_targets.reshape(-1)
    flat = jnp.where(flat < 0, n_local, flat)
    slots = flat.shape[0]
    ids = jnp.arange(slots, dtype=jnp.int32)
    before = (flat[None, :] < flat[:, None]) | (
        (flat[None, :] == flat[:, None]) & (ids[None, :] < ids[:, None])
    )
    rank = jnp.sum(before, axis=1, dtype=jnp.int32)
    order = jnp.sum((rank[None, :] == ids[:, None]) * ids[None, :], axis=1, dtype=jnp.int32)
    start = jnp.sum(
        flat[None, :] < jnp.arange(n_local + 1, dtype=jnp.int32)[:, None], axis=1, dtype=jnp.int32
    )
    where = jnp.stack(
        [row_index * row_tiles, col_index, jnp.full((), col_blocks * halves, jnp.int32)]
    ).astype(jnp.int32)

    whole = pl.BlockSpec(memory_space=pltpu.VMEM)
    own_panel = pl.pallas_call(
        functools.partial(panel_kernel, halves),
        out_shape=jax.ShapeDtypeStruct((row_tiles, halves, tile_rows, tile_cols), jnp.float32),
        grid_spec=pltpu.PrefetchScalarGridSpec(
            num_scalar_prefetch=3,
            grid=(row_tiles,),
            in_specs=[whole, whole],
            out_specs=pl.BlockSpec(
                (1, halves, tile_rows, tile_cols), lambda t, *_: (t, 0, 0, 0)
            ),
        ),
        compiler_params=pltpu.CompilerParams(vmem_limit_bytes=52 * 2**20),
    )(order, start, where, arrived, front_diagonal)

    pieces = 12
    anywhere = pl.BlockSpec(memory_space=pl.ANY)
    panels, rows = pl.pallas_call(
        functools.partial(chain_kernel, n_row, n_col, col_blocks, pieces),
        out_shape=(
            jax.ShapeDtypeStruct(
                (SECTIONS, row_tiles, halves, tile_rows, tile_cols), jnp.float32
            ),
            jax.ShapeDtypeStruct(
                (col_blocks, SECTIONS, halves, tile_rows, tile_cols), jnp.float32
            ),
        ),
        in_specs=[anywhere],
        out_specs=(anywhere, anywhere),
        scratch_shapes=[
            pltpu.SemaphoreType.DMA,
            pltpu.SemaphoreType.DMA((SECTIONS, 2, pieces)),
            pltpu.SemaphoreType.DMA((SECTIONS, pieces)),
            pltpu.SemaphoreType.DMA((col_blocks, SECTIONS, n_row)),
            pltpu.SemaphoreType.DMA((col_blocks, SECTIONS)),
        ],
        compiler_params=pltpu.CompilerParams(collective_id=0, has_side_effects=True),
    )(own_panel)

    rows = rows.transpose(0, 3, 1, 2, 4).reshape(col_blocks * panel_width, wide)
    weight = -mm(gram, rows.T)
    first = jnp.where(col_index < SECTIONS, own_weight, weight[:, :panel_width])
    weight = jnp.concatenate([first, weight[:, panel_width:]], axis=1)
    weight_hi = weight.astype(jnp.bfloat16)
    weight_lo = (weight - weight_hi.astype(jnp.float32)).astype(jnp.bfloat16)

    group = col_blocks * halves
    out = pl.pallas_call(
        functools.partial(final_kernel, col_blocks, halves, n_col),
        out_shape=jax.ShapeDtypeStruct((local_rows * group, tile_cols), jnp.float32),
        grid_spec=pltpu.PrefetchScalarGridSpec(
            num_scalar_prefetch=3,
            grid=(row_tiles,),
            in_specs=[
                whole,
                whole,
                pl.BlockSpec(
                    (SECTIONS, 1, halves, tile_rows, tile_cols), lambda t, *_: (0, t, 0, 0, 0)
                ),
                whole,
                whole,
                whole,
                whole,
            ],
            out_specs=pl.BlockSpec((tile_rows * group, tile_cols), lambda t, *_: (t, 0)),
            scratch_shapes=[pltpu.VMEM((tile_rows, wide), jnp.float32)],
        ),
        compiler_params=pltpu.CompilerParams(vmem_limit_bytes=52 * 2**20),
    )(order, start, where, arrived, front_diagonal, panels, weight_hi, weight_lo, top, own_top)
    out = out.reshape(local_rows, halves, col_blocks, tile_cols).transpose(0, 2, 1, 3)
    return out.reshape(local_rows, col_blocks, panel_width)


def solution(mesh):
    in_specs = (
        P(("row", "col"), None, None),
        P(("row", "col")),
        P(("row", "col"), None),
        P(("row", "col")),
        P(None, "col"),
    )
    out_specs = P("row", None, "col")
    return jax.shard_map(
        functools.partial(on_device, mesh.shape["row"], mesh.shape["col"]),
        mesh=mesh,
        in_specs=in_specs,
        out_specs=out_specs,
        check_vma=False,
    )
```

```python
import functools

import jax
import jax.numpy as jnp
from jax import lax
from jax.experimental import pallas as pl
from jax.experimental.pallas import tpu as pltpu
from jax.sharding import PartitionSpec as P

NF = 49152
CAP = 2
SECTIONS = 2
HI = lax.Precision.HIGHEST
MESH = pl.DeviceIdType.MESH


def mm(a, b):
    return jnp.dot(a, b, precision=HI)


def add_tiles(order_ref, start_ref, arrived_ref, position, shape):
    first = start_ref[position]
    last = start_ref[position + 1]
    return lax.fori_loop(
        first, last, lambda i, acc: acc + arrived_ref[order_ref[i]], jnp.zeros(shape, jnp.float32)
    )


def diagonal_tile(diag_row, half, shape):
    rows = lax.broadcasted_iota(jnp.int32, shape, 0)
    cols = lax.broadcasted_iota(jnp.int32, shape, 1) + half * shape[1]
    return jnp.where(rows == cols, diag_row, 0.0)


def panel_kernel(halves, order_ref, start_ref, where_ref, arrived_ref, diag_ref, out_ref):
    step = pl.program_id(0)
    shape = out_ref.shape[2:]
    base = where_ref[0] + step

    @pl.when(where_ref[1] < SECTIONS)
    def _():
        for half in range(halves):
            out_ref[0, half] = add_tiles(
                order_ref, start_ref, arrived_ref, step * where_ref[2] + half, shape
            )

        @pl.when(base == where_ref[1])
        def _():
            for half in range(halves):
                diag_row = diag_ref[0:1, half * shape[1] : (half + 1) * shape[1]]
                out_ref[0, half] += diagonal_tile(diag_row, half, shape)


def chain_kernel(n_row, n_col, col_blocks, pieces, own_ref, all_ref, rows_ref, copy_sem, send_sem, recv_sem, rsend_sem, rrecv_sem):
    row = lax.axis_index("row")
    col = lax.axis_index("col")
    row_tiles = own_ref.shape[0]
    per = row_tiles // pieces
    barrier = pltpu.get_barrier_semaphore()
    for step in (1, n_col - 1):
        pl.semaphore_signal(
            barrier, inc=1, device_id={"col": lax.rem(col + step, n_col)}, device_id_type=MESH
        )
    for shift in range(1, n_row):
        pl.semaphore_signal(
            barrier,
            inc=1,
            device_id={"row": lax.rem(row + shift, n_row)},
            device_id_type=MESH,
        )
    pl.semaphore_wait(barrier, n_row + 1)

    def part(ref, piece):
        return ref.at[pl.ds(piece * per, per)]

    def distance(section, piece):
        if piece % 2 == 0:
            return lax.rem(col - section + n_col, n_col)
        return lax.rem(section - col + n_col, n_col)

    def hop(section, piece, from_own):
        step = 1 if piece % 2 == 0 else n_col - 1
        target = all_ref.at[section]
        source = own_ref if from_own else target
        return pltpu.make_async_remote_copy(
            src_ref=part(source, piece),
            dst_ref=part(target, piece),
            send_sem=send_sem.at[section, piece],
            recv_sem=recv_sem.at[section, piece],
            device_id={"col": lax.rem(col + step, n_col)},
            device_id_type=MESH,
        )

    def local(section):
        return pltpu.make_async_copy(own_ref, all_ref.at[section], copy_sem)

    for section in range(SECTIONS):

        @pl.when(col == section)
        def _():
            for piece in range(pieces):
                hop(section, piece, True).start()
            local(section).start()
            local(section).wait()

    def row_copy(block, section, shift):
        tile = block * n_col + col
        return pltpu.make_async_remote_copy(
            src_ref=all_ref.at[section, lax.rem(tile, row_tiles)],
            dst_ref=rows_ref.at[block, section],
            send_sem=rsend_sem.at[block, section, shift],
            recv_sem=rrecv_sem.at[block, section],
            device_id={"row": lax.rem(row + shift, n_row)},
            device_id_type=MESH,
        )

    def row_local(block, section):
        tile = block * n_col + col
        return pltpu.make_async_copy(
            all_ref.at[section, lax.rem(tile, row_tiles)],
            rows_ref.at[block, section],
            rsend_sem.at[block, section, 0],
        )

    def owner(block):
        return row == (block * n_col + col) // row_tiles

    needed = min(col_blocks * n_col, row_tiles)
    send_rows_at = -(-needed // per) - 1
    for piece in range(pieces):
        for section in range(SECTIONS):

            @pl.when(col != section)
            def _():
                hop(section, piece, False).wait_recv()

            @pl.when(jnp.logical_and(col != section, distance(section, piece) < n_col - 1))
            def _():
                hop(section, piece, False).start()

        if piece == send_rows_at:
            for block in range(col_blocks):

                @pl.when(owner(block))
                def _():
                    for section in range(SECTIONS):
                        for shift in range(1, n_row):
                            row_copy(block, section, shift).start()
                        row_local(block, section).start()

    for block in range(col_blocks):

        @pl.when(owner(block))
        def _():
            for section in range(SECTIONS):
                for shift in range(1, n_row):
                    row_copy(block, section, shift).wait_send()
                row_local(block, section).wait()

        @pl.when(jnp.logical_not(owner(block)))
        def _():
            for section in range(SECTIONS):
                row_copy(block, section, 1).wait_recv()

    for section in range(SECTIONS):
        for piece in range(pieces):

            @pl.when(distance(section, piece) < n_col - 1)
            def _():
                hop(section, piece, False).wait_send()


def final_kernel(col_blocks, halves, n_col, order_ref, start_ref, where_ref, arrived_ref, diag_ref, panels_ref, whi_ref, wlo_ref, top_ref, own_ref, out_ref, lhs_ref):
    step = pl.program_id(0)
    rows, lanes = arrived_ref.shape[1:]
    width = halves * lanes
    base = where_ref[0] + step
    for section in range(SECTIONS):
        for half in range(halves):
            low = section * width + half * lanes
            lhs_ref[:, low : low + lanes] = panels_ref[section, 0, half]

    @pl.when(base < SECTIONS)
    def _():
        lhs_ref[...] = top_ref[jnp.minimum(base, SECTIONS - 1)]

    lhs = lhs_ref[...]
    hi = lhs.astype(jnp.bfloat16)
    lo = (lhs - hi.astype(jnp.float32)).astype(jnp.bfloat16)
    whi = whi_ref[...]
    product = (
        jnp.dot(hi, wlo_ref[...], preferred_element_type=jnp.float32)
        + jnp.dot(lo, whi, preferred_element_type=jnp.float32)
    ) + jnp.dot(hi, whi, preferred_element_type=jnp.float32)
    panel_column = where_ref[1] < SECTIONS
    group = col_blocks * halves
    for block in range(col_blocks):
        for half in range(halves):
            low = block * width + half * lanes
            value = product[:, low : low + lanes]
            slot = half * col_blocks + block
            place = (pl.ds(slot, rows, stride=group), slice(None))

            def trailing():
                position = step * group + block * halves + half
                out_ref[place] = value + add_tiles(
                    order_ref, start_ref, arrived_ref, position, (rows, lanes)
                )

                @pl.when(base == block * n_col + where_ref[1])
                def _():
                    diag_row = diag_ref[block : block + 1, half * lanes : (half + 1) * lanes]
                    out_ref[place] = out_ref[place] + diagonal_tile(diag_row, half, (rows, lanes))

            if block > 0:
                trailing()
            else:
                pl.when(jnp.logical_not(panel_column))(trailing)

                @pl.when(panel_column)
                def _():
                    out_ref[place] = value

                @pl.when(jnp.logical_and(panel_column, base < SECTIONS))
                def _():
                    out_ref[place] = own_ref[
                        jnp.minimum(base, SECTIONS - 1), :, half * lanes : (half + 1) * lanes
                    ]


def on_device(n_row, n_col, child_tiles, tile_dest, tile_mask, tile_count, front_diagonal):
    devices = n_row * n_col
    row_index = lax.axis_index("row")
    col_index = lax.axis_index("col")
    tile_total, tile_rows, tile_cols = child_tiles.shape
    col_blocks, panel_width = front_diagonal.shape
    halves = panel_width // tile_cols
    local_rows = NF // n_row
    row_tiles = local_rows // tile_rows
    col_tiles = col_blocks * n_col * halves
    is_live = jnp.arange(tile_total, dtype=jnp.int32) < tile_count[0]
    row_tile = tile_dest // col_tiles
    col_tile = tile_dest % col_tiles
    col_block = col_tile // halves
    col_half = col_tile % halves
    owner_row = row_tile // row_tiles
    owner_dev = jnp.where(is_live, owner_row * n_col + col_block % n_col, devices)
    local_tile = (
        (row_tile - owner_row * row_tiles) * (col_blocks * halves)
        + col_block // n_col * halves
        + col_half
    )
    earlier = jnp.tril(jnp.ones((tile_total, tile_total), jnp.int32), -1)
    slot_rank = jnp.sum((owner_dev[:, None] == owner_dev[None, :]) * earlier, axis=1)
    position = jnp.where(is_live, owner_dev * CAP + slot_rank, devices * CAP)
    hit = position[None, :] == jnp.arange(devices * CAP, dtype=jnp.int32)[:, None]
    source = jnp.sum(
        hit * jnp.arange(tile_total, dtype=jnp.int32)[None, :], axis=1, dtype=jnp.int32
    )
    targets = jnp.sum(hit * (local_tile + 1)[None, :], axis=1, dtype=jnp.int32) - 1
    masked = child_tiles * tile_mask.astype(jnp.float32)[:, :, None]
    outgoing = masked[source]
    wide = SECTIONS * panel_width
    in_pivot = is_live & (row_tile < SECTIONS) & (col_tile < (row_tile + 1) * halves)
    pivot_block = row_tile * (row_tile + 1) // 2 + col_block
    pivot_count = SECTIONS * (SECTIONS + 1) // 2
    pivot_slot = jnp.where(in_pivot, pivot_block * halves + col_half, pivot_count * halves)
    pivot = jax.ops.segment_sum(masked, pivot_slot, num_segments=pivot_count * halves + 1)
    pivot = pivot[: pivot_count * halves].reshape(pivot_count, halves, tile_rows, tile_cols)
    pivot = pivot.transpose(0, 2, 1, 3).reshape(pivot_count, tile_rows, panel_width)
    own_diag = jnp.where(
        (jnp.arange(pivot_count) == col_index * (col_index + 3) // 2) & (row_index == 0), 1.0, 0.0
    )
    pivot = pivot + own_diag[:, None, None] * jnp.diag(front_diagonal[0])[None]
    pivot = lax.psum(pivot, ("row", "col"))
    pivot, outgoing = lax.optimization_barrier((pivot, outgoing))
    arrived_targets = lax.all_to_all(
        targets.reshape(devices, CAP), ("row", "col"), split_axis=0, concat_axis=0, tiled=True
    )
    arrived = lax.all_to_all(
        outgoing.reshape(devices, CAP, tile_rows, tile_cols),
        ("row", "col"),
        split_axis=0,
        concat_axis=0,
        tiled=True,
    ).reshape(-1, tile_rows, tile_cols)

    eye = jnp.eye(panel_width, dtype=jnp.float32)
    b00, b10, b11 = pivot
    b00 = 0.5 * (b00 + b00.T)
    b11 = 0.5 * (b11 + b11.T)
    l00 = jnp.linalg.cholesky(b00)
    x0 = jax.scipy.linalg.solve_triangular(l00, eye, lower=True)
    l10 = mm(b10, x0.T)
    l11 = jnp.linalg.cholesky(b11 - mm(l10, l10.T))
    x1 = jax.scipy.linalg.solve_triangular(l11, eye, lower=True)
    zero = jnp.zeros_like(eye)
    inverse = jnp.block([[x0, zero], [-mm(x1, mm(l10, x0)), x1]])
    full = jnp.block([[l00, zero], [l10, l11]])
    top = jnp.block([[b00, b10.T], [b10, b11]]).reshape(SECTIONS, tile_rows, wide)
    gram = mm(inverse.T, inverse)
    section_at = jnp.minimum(col_index, SECTIONS - 1) * panel_width
    own_top = lax.dynamic_slice_in_dim(full, section_at, panel_width, axis=1)
    own_top = own_top.reshape(SECTIONS, tile_rows, panel_width)
    own_weight = lax.dynamic_slice_in_dim(inverse, section_at, panel_width, axis=0).T

    n_local = row_tiles * col_blocks * halves
    flat = arrived_targets.reshape(-1)
    flat = jnp.where(flat < 0, n_local, flat)
    slots = flat.shape[0]
    ids = jnp.arange(slots, dtype=jnp.int32)
    before = (flat[None, :] < flat[:, None]) | (
        (flat[None, :] == flat[:, None]) & (ids[None, :] < ids[:, None])
    )
    rank = jnp.sum(before, axis=1, dtype=jnp.int32)
    order = jnp.sum((rank[None, :] == ids[:, None]) * ids[None, :], axis=1, dtype=jnp.int32)
    start = jnp.sum(
        flat[None, :] < jnp.arange(n_local + 1, dtype=jnp.int32)[:, None], axis=1, dtype=jnp.int32
    )
    where = jnp.stack(
        [row_index * row_tiles, col_index, jnp.full((), col_blocks * halves, jnp.int32)]
    ).astype(jnp.int32)

    whole = pl.BlockSpec(memory_space=pltpu.VMEM)
    own_panel = pl.pallas_call(
        functools.partial(panel_kernel, halves),
        out_shape=jax.ShapeDtypeStruct((row_tiles, halves, tile_rows, tile_cols), jnp.float32),
        grid_spec=pltpu.PrefetchScalarGridSpec(
            num_scalar_prefetch=3,
            grid=(row_tiles,),
            in_specs=[whole, whole],
            out_specs=pl.BlockSpec(
                (1, halves, tile_rows, tile_cols), lambda t, *_: (t, 0, 0, 0)
            ),
        ),
        compiler_params=pltpu.CompilerParams(vmem_limit_bytes=52 * 2**20),
    )(order, start, where, arrived, front_diagonal)

    pieces = 12
    anywhere = pl.BlockSpec(memory_space=pl.ANY)
    panels, rows = pl.pallas_call(
        functools.partial(chain_kernel, n_row, n_col, col_blocks, pieces),
        out_shape=(
            jax.ShapeDtypeStruct(
                (SECTIONS, row_tiles, halves, tile_rows, tile_cols), jnp.float32
            ),
            jax.ShapeDtypeStruct(
                (col_blocks, SECTIONS, halves, tile_rows, tile_cols), jnp.float32
            ),
        ),
        in_specs=[anywhere],
        out_specs=(anywhere, anywhere),
        scratch_shapes=[
            pltpu.SemaphoreType.DMA,
            pltpu.SemaphoreType.DMA((SECTIONS, pieces)),
            pltpu.SemaphoreType.DMA((SECTIONS, pieces)),
            pltpu.SemaphoreType.DMA((col_blocks, SECTIONS, n_row)),
            pltpu.SemaphoreType.DMA((col_blocks, SECTIONS)),
        ],
        compiler_params=pltpu.CompilerParams(collective_id=0, has_side_effects=True),
    )(own_panel)

    rows = rows.transpose(0, 3, 1, 2, 4).reshape(col_blocks * panel_width, wide)
    weight = -mm(gram, rows.T)
    first = jnp.where(col_index < SECTIONS, own_weight, weight[:, :panel_width])
    weight = jnp.concatenate([first, weight[:, panel_width:]], axis=1)
    weight_hi = weight.astype(jnp.bfloat16)
    weight_lo = (weight - weight_hi.astype(jnp.float32)).astype(jnp.bfloat16)

    group = col_blocks * halves
    out = pl.pallas_call(
        functools.partial(final_kernel, col_blocks, halves, n_col),
        out_shape=jax.ShapeDtypeStruct((local_rows * group, tile_cols), jnp.float32),
        grid_spec=pltpu.PrefetchScalarGridSpec(
            num_scalar_prefetch=3,
            grid=(row_tiles,),
            in_specs=[
                whole,
                whole,
                pl.BlockSpec(
                    (SECTIONS, 1, halves, tile_rows, tile_cols), lambda t, *_: (0, t, 0, 0, 0)
                ),
                whole,
                whole,
                whole,
                whole,
            ],
            out_specs=pl.BlockSpec((tile_rows * group, tile_cols), lambda t, *_: (t, 0)),
            scratch_shapes=[pltpu.VMEM((tile_rows, wide), jnp.float32)],
        ),
        compiler_params=pltpu.CompilerParams(vmem_limit_bytes=52 * 2**20),
    )(order, start, where, arrived, front_diagonal, panels, weight_hi, weight_lo, top, own_top)
    out = out.reshape(local_rows, halves, col_blocks, tile_cols).transpose(0, 2, 1, 3)
    return out.reshape(local_rows, col_blocks, panel_width)


def solution(mesh):
    in_specs = (
        P(("row", "col"), None, None),
        P(("row", "col")),
        P(("row", "col"), None),
        P(("row", "col")),
        P(None, "col"),
    )
    out_specs = P("row", None, "col")
    return jax.shard_map(
        functools.partial(on_device, mesh.shape["row"], mesh.shape["col"]),
        mesh=mesh,
        in_specs=in_specs,
        out_specs=out_specs,
        check_vma=False,
    )
```

```python
import functools

import jax
import jax.numpy as jnp
from jax import lax
from jax.experimental import pallas as pl
from jax.experimental.pallas import tpu as pltpu
from jax.sharding import PartitionSpec as P

NF = 49152
CAP = 2
SECTIONS = 2
HI = lax.Precision.HIGHEST
MESH = pl.DeviceIdType.MESH


def mm(a, b):
    return jnp.dot(a, b, precision=HI)


def add_tiles(order_ref, start_ref, arrived_ref, position, shape):
    first = start_ref[position]
    last = start_ref[position + 1]
    return lax.fori_loop(
        first, last, lambda i, acc: acc + arrived_ref[order_ref[i]], jnp.zeros(shape, jnp.float32)
    )


def diagonal_tile(diag_row, half, shape):
    rows = lax.broadcasted_iota(jnp.int32, shape, 0)
    cols = lax.broadcasted_iota(jnp.int32, shape, 1) + half * shape[1]
    return jnp.where(rows == cols, diag_row, 0.0)


def panel_kernel(halves, order_ref, start_ref, where_ref, arrived_ref, diag_ref, out_ref):
    step = pl.program_id(0)
    shape = out_ref.shape[2:]
    base = where_ref[0] + step

    @pl.when(where_ref[1] < SECTIONS)
    def _():
        for half in range(halves):
            out_ref[0, half] = add_tiles(
                order_ref, start_ref, arrived_ref, step * where_ref[2] + half, shape
            )

        @pl.when(base == where_ref[1])
        def _():
            for half in range(halves):
                diag_row = diag_ref[0:1, half * shape[1] : (half + 1) * shape[1]]
                out_ref[0, half] += diagonal_tile(diag_row, half, shape)


def chain_kernel(n_row, n_col, col_blocks, pieces, own_ref, all_ref, rows_ref, copy_sem, send_sem, recv_sem, rsend_sem, rrecv_sem):
    row = lax.axis_index("row")
    col = lax.axis_index("col")
    row_tiles = own_ref.shape[0]
    per = row_tiles // pieces
    barrier = pltpu.get_barrier_semaphore()
    for step in (1, -1):
        inside = (col < n_col - 1) if step == 1 else (col > 0)

        @pl.when(inside)
        def _():
            pl.semaphore_signal(
                barrier, inc=1, device_id={"col": col + step}, device_id_type=MESH
            )

    for shift in range(1, n_row):
        pl.semaphore_signal(
            barrier,
            inc=1,
            device_id={"row": lax.rem(row + shift, n_row)},
            device_id_type=MESH,
        )

    at_end = jnp.logical_or(col == 0, col == n_col - 1)

    @pl.when(at_end)
    def _():
        pl.semaphore_wait(barrier, n_row)

    @pl.when(jnp.logical_not(at_end))
    def _():
        pl.semaphore_wait(barrier, n_row + 1)

    def part(ref, piece):
        return ref.at[pl.ds(piece * per, per)]

    def hop(section, piece, step, from_own):
        target = all_ref.at[section]
        source = own_ref if from_own else target
        way = 0 if step == 1 else 1
        return pltpu.make_async_remote_copy(
            src_ref=part(source, piece),
            dst_ref=part(target, piece),
            send_sem=send_sem.at[section, way, piece],
            recv_sem=recv_sem.at[section, piece],
            device_id={"col": col + step},
            device_id_type=MESH,
        )

    def local(section):
        return pltpu.make_async_copy(own_ref, all_ref.at[section], copy_sem)

    for section in range(SECTIONS):

        @pl.when(col == section)
        def _():
            local(section).start()
            if section == 0:
                for piece in range(pieces):
                    hop(section, piece, 1, True).start()
            local(section).wait()

    def row_copy(block, section, shift):
        tile = block * n_col + col
        return pltpu.make_async_remote_copy(
            src_ref=all_ref.at[section, lax.rem(tile, row_tiles)],
            dst_ref=rows_ref.at[block, section],
            send_sem=rsend_sem.at[block, section, shift],
            recv_sem=rrecv_sem.at[block, section],
            device_id={"row": lax.rem(row + shift, n_row)},
            device_id_type=MESH,
        )

    def row_local(block, section):
        tile = block * n_col + col
        return pltpu.make_async_copy(
            all_ref.at[section, lax.rem(tile, row_tiles)],
            rows_ref.at[block, section],
            rsend_sem.at[block, section, 0],
        )

    def owner(block):
        return row == (block * n_col + col) // row_tiles

    needed = min(col_blocks * n_col, row_tiles)
    send_rows_at = -(-needed // per) - 1
    copies = [(section, shift) for shift in range(1, n_row) for section in range(SECTIONS)]
    batch = -(-len(copies) // (pieces - send_rows_at))
    odd = lax.rem(row, 2) == 1
    for piece in range(pieces):
        for section in range(1, SECTIONS):

            @pl.when(jnp.logical_and(col == section, jnp.logical_not(odd)))
            def _():
                hop(section, piece, -1, True).start()

            @pl.when(jnp.logical_and(col == section, col < n_col - 1))
            def _():
                hop(section, piece, 1, True).start()

        for section in range(SECTIONS):

            @pl.when(col != section)
            def _():
                hop(section, piece, 1, False).wait_recv()

            if section < n_col - 1:

                @pl.when(jnp.logical_and(col > section, col < n_col - 1))
                def _():
                    hop(section, piece, 1, False).start()

            if section > 1:

                @pl.when(jnp.logical_and(col < section, col > 0))
                def _():
                    hop(section, piece, -1, False).start()

        for section in range(1, SECTIONS):

            @pl.when(jnp.logical_and(col == section, odd))
            def _():
                hop(section, piece, -1, True).start()

        if piece >= send_rows_at:
            low = (piece - send_rows_at) * batch
            for block in range(col_blocks):

                @pl.when(owner(block))
                def _():
                    if piece == send_rows_at:
                        for section in range(SECTIONS):
                            row_local(block, section).start()
                    for section, shift in copies[low : low + batch]:
                        row_copy(block, section, shift).start()

    for block in range(col_blocks):

        @pl.when(owner(block))
        def _():
            for section in range(SECTIONS):
                for shift in range(1, n_row):
                    row_copy(block, section, shift).wait_send()
                row_local(block, section).wait()

        @pl.when(jnp.logical_not(owner(block)))
        def _():
            for section in range(SECTIONS):
                row_copy(block, section, 1).wait_recv()

    for section in range(SECTIONS):
        for piece in range(pieces):

            @pl.when(jnp.logical_and(col >= section, col < n_col - 1))
            def _():
                hop(section, piece, 1, False).wait_send()

            if section > 0:

                @pl.when(jnp.logical_and(col <= section, col > 0))
                def _():
                    hop(section, piece, -1, False).wait_send()


def final_kernel(col_blocks, halves, n_col, order_ref, start_ref, where_ref, arrived_ref, diag_ref, panels_ref, whi_ref, wlo_ref, top_ref, own_ref, out_ref, lhs_ref):
    step = pl.program_id(0)
    rows, lanes = arrived_ref.shape[1:]
    width = halves * lanes
    base = where_ref[0] + step
    for section in range(SECTIONS):
        for half in range(halves):
            low = section * width + half * lanes
            lhs_ref[:, low : low + lanes] = panels_ref[section, 0, half]

    @pl.when(base < SECTIONS)
    def _():
        lhs_ref[...] = top_ref[jnp.minimum(base, SECTIONS - 1)]

    lhs = lhs_ref[...]
    hi = lhs.astype(jnp.bfloat16)
    lo = (lhs - hi.astype(jnp.float32)).astype(jnp.bfloat16)
    whi = whi_ref[...]
    product = (
        jnp.dot(hi, wlo_ref[...], preferred_element_type=jnp.float32)
        + jnp.dot(lo, whi, preferred_element_type=jnp.float32)
    ) + jnp.dot(hi, whi, preferred_element_type=jnp.float32)
    panel_column = where_ref[1] < SECTIONS
    group = col_blocks * halves
    for block in range(col_blocks):
        for half in range(halves):
            low = block * width + half * lanes
            value = product[:, low : low + lanes]
            slot = half * col_blocks + block
            place = (pl.ds(slot, rows, stride=group), slice(None))

            def trailing():
                position = step * group + block * halves + half
                out_ref[place] = value + add_tiles(
                    order_ref, start_ref, arrived_ref, position, (rows, lanes)
                )

                @pl.when(base == block * n_col + where_ref[1])
                def _():
                    diag_row = diag_ref[block : block + 1, half * lanes : (half + 1) * lanes]
                    out_ref[place] = out_ref[place] + diagonal_tile(diag_row, half, (rows, lanes))

            if block > 0:
                trailing()
            else:
                pl.when(jnp.logical_not(panel_column))(trailing)

                @pl.when(panel_column)
                def _():
                    out_ref[place] = value

                @pl.when(jnp.logical_and(panel_column, base < SECTIONS))
                def _():
                    out_ref[place] = own_ref[
                        jnp.minimum(base, SECTIONS - 1), :, half * lanes : (half + 1) * lanes
                    ]


def on_device(n_row, n_col, child_tiles, tile_dest, tile_mask, tile_count, front_diagonal):
    devices = n_row * n_col
    row_index = lax.axis_index("row")
    col_index = lax.axis_index("col")
    tile_total, tile_rows, tile_cols = child_tiles.shape
    col_blocks, panel_width = front_diagonal.shape
    halves = panel_width // tile_cols
    local_rows = NF // n_row
    row_tiles = local_rows // tile_rows
    col_tiles = col_blocks * n_col * halves
    is_live = jnp.arange(tile_total, dtype=jnp.int32) < tile_count[0]
    row_tile = tile_dest // col_tiles
    col_tile = tile_dest % col_tiles
    col_block = col_tile // halves
    col_half = col_tile % halves
    owner_row = row_tile // row_tiles
    owner_dev = jnp.where(is_live, owner_row * n_col + col_block % n_col, devices)
    local_tile = (
        (row_tile - owner_row * row_tiles) * (col_blocks * halves)
        + col_block // n_col * halves
        + col_half
    )
    earlier = jnp.tril(jnp.ones((tile_total, tile_total), jnp.int32), -1)
    slot_rank = jnp.sum((owner_dev[:, None] == owner_dev[None, :]) * earlier, axis=1)
    position = jnp.where(is_live, owner_dev * CAP + slot_rank, devices * CAP)
    hit = position[None, :] == jnp.arange(devices * CAP, dtype=jnp.int32)[:, None]
    source = jnp.sum(
        hit * jnp.arange(tile_total, dtype=jnp.int32)[None, :], axis=1, dtype=jnp.int32
    )
    targets = jnp.sum(hit * (local_tile + 1)[None, :], axis=1, dtype=jnp.int32) - 1
    masked = child_tiles * tile_mask.astype(jnp.float32)[:, :, None]
    outgoing = masked[source]
    wide = SECTIONS * panel_width
    in_pivot = is_live & (row_tile < SECTIONS) & (col_tile < (row_tile + 1) * halves)
    pivot_block = row_tile * (row_tile + 1) // 2 + col_block
    pivot_count = SECTIONS * (SECTIONS + 1) // 2
    pivot_slot = jnp.where(in_pivot, pivot_block * halves + col_half, pivot_count * halves)
    pivot = jax.ops.segment_sum(masked, pivot_slot, num_segments=pivot_count * halves + 1)
    pivot = pivot[: pivot_count * halves].reshape(pivot_count, halves, tile_rows, tile_cols)
    pivot = pivot.transpose(0, 2, 1, 3).reshape(pivot_count, tile_rows, panel_width)
    own_diag = jnp.where(
        (jnp.arange(pivot_count) == col_index * (col_index + 3) // 2) & (row_index == 0), 1.0, 0.0
    )
    pivot = pivot + own_diag[:, None, None] * jnp.diag(front_diagonal[0])[None]
    pivot = lax.psum(pivot, ("row", "col"))
    pivot, outgoing = lax.optimization_barrier((pivot, outgoing))
    arrived_targets = lax.all_to_all(
        targets.reshape(devices, CAP), ("row", "col"), split_axis=0, concat_axis=0, tiled=True
    )
    arrived = lax.all_to_all(
        outgoing.reshape(devices, CAP, tile_rows, tile_cols),
        ("row", "col"),
        split_axis=0,
        concat_axis=0,
        tiled=True,
    ).reshape(-1, tile_rows, tile_cols)

    eye = jnp.eye(panel_width, dtype=jnp.float32)
    b00, b10, b11 = pivot
    b00 = 0.5 * (b00 + b00.T)
    b11 = 0.5 * (b11 + b11.T)
    l00 = jnp.linalg.cholesky(b00)
    x0 = jax.scipy.linalg.solve_triangular(l00, eye, lower=True)
    l10 = mm(b10, x0.T)
    l11 = jnp.linalg.cholesky(b11 - mm(l10, l10.T))
    x1 = jax.scipy.linalg.solve_triangular(l11, eye, lower=True)
    zero = jnp.zeros_like(eye)
    inverse = jnp.block([[x0, zero], [-mm(x1, mm(l10, x0)), x1]])
    full = jnp.block([[l00, zero], [l10, l11]])
    top = jnp.block([[b00, b10.T], [b10, b11]]).reshape(SECTIONS, tile_rows, wide)
    gram = mm(inverse.T, inverse)
    section_at = jnp.minimum(col_index, SECTIONS - 1) * panel_width
    own_top = lax.dynamic_slice_in_dim(full, section_at, panel_width, axis=1)
    own_top = own_top.reshape(SECTIONS, tile_rows, panel_width)
    own_weight = lax.dynamic_slice_in_dim(inverse, section_at, panel_width, axis=0).T

    n_local = row_tiles * col_blocks * halves
    flat = arrived_targets.reshape(-1)
    flat = jnp.where(flat < 0, n_local, flat)
    slots = flat.shape[0]
    ids = jnp.arange(slots, dtype=jnp.int32)
    before = (flat[None, :] < flat[:, None]) | (
        (flat[None, :] == flat[:, None]) & (ids[None, :] < ids[:, None])
    )
    rank = jnp.sum(before, axis=1, dtype=jnp.int32)
    order = jnp.sum((rank[None, :] == ids[:, None]) * ids[None, :], axis=1, dtype=jnp.int32)
    start = jnp.sum(
        flat[None, :] < jnp.arange(n_local + 1, dtype=jnp.int32)[:, None], axis=1, dtype=jnp.int32
    )
    where = jnp.stack(
        [row_index * row_tiles, col_index, jnp.full((), col_blocks * halves, jnp.int32)]
    ).astype(jnp.int32)

    whole = pl.BlockSpec(memory_space=pltpu.VMEM)
    own_panel = pl.pallas_call(
        functools.partial(panel_kernel, halves),
        out_shape=jax.ShapeDtypeStruct((row_tiles, halves, tile_rows, tile_cols), jnp.float32),
        grid_spec=pltpu.PrefetchScalarGridSpec(
            num_scalar_prefetch=3,
            grid=(row_tiles,),
            in_specs=[whole, whole],
            out_specs=pl.BlockSpec(
                (1, halves, tile_rows, tile_cols), lambda t, *_: (t, 0, 0, 0)
            ),
        ),
        compiler_params=pltpu.CompilerParams(vmem_limit_bytes=52 * 2**20),
    )(order, start, where, arrived, front_diagonal)

    pieces = 12
    anywhere = pl.BlockSpec(memory_space=pl.ANY)
    panels, rows = pl.pallas_call(
        functools.partial(chain_kernel, n_row, n_col, col_blocks, pieces),
        out_shape=(
            jax.ShapeDtypeStruct(
                (SECTIONS, row_tiles, halves, tile_rows, tile_cols), jnp.float32
            ),
            jax.ShapeDtypeStruct(
                (col_blocks, SECTIONS, halves, tile_rows, tile_cols), jnp.float32
            ),
        ),
        in_specs=[anywhere],
        out_specs=(anywhere, anywhere),
        scratch_shapes=[
            pltpu.SemaphoreType.DMA,
            pltpu.SemaphoreType.DMA((SECTIONS, 2, pieces)),
            pltpu.SemaphoreType.DMA((SECTIONS, pieces)),
            pltpu.SemaphoreType.DMA((col_blocks, SECTIONS, n_row)),
            pltpu.SemaphoreType.DMA((col_blocks, SECTIONS)),
        ],
        compiler_params=pltpu.CompilerParams(collective_id=0, has_side_effects=True),
    )(own_panel)

    rows = rows.transpose(0, 3, 1, 2, 4).reshape(col_blocks * panel_width, wide)
    weight = -mm(gram, rows.T)
    first = jnp.where(col_index < SECTIONS, own_weight, weight[:, :panel_width])
    weight = jnp.concatenate([first, weight[:, panel_width:]], axis=1)
    weight_hi = weight.astype(jnp.bfloat16)
    weight_lo = (weight - weight_hi.astype(jnp.float32)).astype(jnp.bfloat16)

    group = col_blocks * halves
    out = pl.pallas_call(
        functools.partial(final_kernel, col_blocks, halves, n_col),
        out_shape=jax.ShapeDtypeStruct((local_rows * group, tile_cols), jnp.float32),
        grid_spec=pltpu.PrefetchScalarGridSpec(
            num_scalar_prefetch=3,
            grid=(row_tiles,),
            in_specs=[
                whole,
                whole,
                pl.BlockSpec(
                    (SECTIONS, 1, halves, tile_rows, tile_cols), lambda t, *_: (0, t, 0, 0, 0)
                ),
                whole,
                whole,
                whole,
                whole,
            ],
            out_specs=pl.BlockSpec((tile_rows * group, tile_cols), lambda t, *_: (t, 0)),
            scratch_shapes=[pltpu.VMEM((tile_rows, wide), jnp.float32)],
        ),
        compiler_params=pltpu.CompilerParams(vmem_limit_bytes=52 * 2**20),
    )(order, start, where, arrived, front_diagonal, panels, weight_hi, weight_lo, top, own_top)
    out = out.reshape(local_rows, halves, col_blocks, tile_cols).transpose(0, 2, 1, 3)
    return out.reshape(local_rows, col_blocks, panel_width)


def solution(mesh):
    in_specs = (
        P(("row", "col"), None, None),
        P(("row", "col")),
        P(("row", "col"), None),
        P(("row", "col")),
        P(None, "col"),
    )
    out_specs = P("row", None, "col")
    return jax.shard_map(
        functools.partial(on_device, mesh.shape["row"], mesh.shape["col"]),
        mesh=mesh,
        in_specs=in_specs,
        out_specs=out_specs,
        check_vma=False,
    )
```
